32 devices in a mesh: slab: 4 (over y, core), tile: 8 (over z, x).
Axes of the slice: x: 2, y: 2, z: 4, core: 2. Of those that a mesh axis runs over, the one named last changes fastest.
Arguments:
- positions: float32 [3, 65536], P(None, ('slab', 'tile')), may hold values from -6 to 6
- radius: float32 [65536], P(('slab', 'tile')), may hold values from 0.7 to 1.4
- uptake_rate: float32 [65536], P(('slab', 'tile')), may hold values from 0.3 to 3
- voxel_local: int32 [65536], P(('slab', 'tile')), may hold values from 0 to 262143
- cell_counts: int32 [32], P(('slab', 'tile')), may hold values from 512 to 2048, as said below
- send_counts: int32 [32, 8], P(('slab', 'tile')), may hold values from 0 to 512, as said below
- neighbor_blocks: int32 [512, 8], P(('slab', 'tile')), may hold values from 0 to 23, as said below
- field: float32 [2, 32, 128, 2048], P(None, 'slab', 'tile'), may hold values from 0.2 to 2
Outputs:
- velocity: float32 [3, 65536], P(None, ('slab', 'tile'))
- field_next: float32 [2, 32, 128, 2048], P(None, 'slab', 'tile')
The draws below stay inside these ranges and needn't reach their ends.
Inputs may be any that keep to these rules, and one draw needn't show every extreme that they name: `cell_counts`: A multiple of 128; in every slab one tile holds 2048 live cells and another 2048 // 4. `send_counts`: row g sums to cell_counts[g]; in every slab all tiles send exactly 512 cells to one common destination tile. `neighbor_blocks`: row g * 16 + b names 8 different blocks of tile g's extended table, the first being 4 + b.
All inputs are finite; a program needn't handle non-finite values.
Results may differ from the reference program's by a relative error of at most 0.0003.
Values sent between devices are 32-bit elements; how exact they have to be, the bound alone decides.
A program may use at most 64 MiB of HBM per device.

```python
import math
import jax
import jax.numpy as jnp
from jax import lax

CZ = 8
CY = 16
NX = 2048
CAP = 2048
HB = 4
K = 8
ITERS = 4
NB = 16
SLOT = 512
NZ = 32
NY = 128
CELLS = 65536
N_SLAB = 4
N_TILE = 8


def count_tables(key):
    base = jax.random.fold_in(key, 7)
    keys = jax.random.split(base, 4)
    quarter = NB // 4
    blocks = jax.random.randint(keys[0], (N_SLAB, N_TILE), quarter, NB + 1)
    full_at = jax.random.randint(keys[1], (N_SLAB, 1), 0, N_TILE)
    low_at = (full_at + 1 + jax.random.randint(keys[2], (N_SLAB, 1), 0, N_TILE - 1)) % N_TILE
    lanes = jnp.arange(N_TILE, dtype=jnp.int32)[None, :]
    blocks = jnp.where(lanes == full_at, NB, jnp.where(lanes == low_at, quarter, blocks))
    living = (blocks * 128).reshape(-1).astype(jnp.int32)
    rows = N_SLAB * N_TILE
    others = N_TILE - 1
    remain = living - SLOT
    even_share = remain // others
    extra = remain % others
    places = jnp.arange(others, dtype=jnp.int32)[None, :]
    shares = even_share[:, None] + (places < extra[:, None]).astype(jnp.int32)
    reach = even_share // 2
    noise = jax.random.randint(keys[3], (rows, others), 0, 1 << 20)
    wobble = noise % (2 * reach[:, None] + 1) - reach[:, None]
    paired = (places % 2 == 0) & (places + 1 < others)
    wobble = jnp.where(paired, wobble, 0)
    shares = shares + wobble - jnp.roll(wobble, 1, axis=1)
    target = jnp.repeat(full_at, N_TILE, axis=0)
    zeros_col = jnp.zeros((rows, 1), jnp.int32)
    before = jnp.concatenate([shares, zeros_col], axis=1)
    after = jnp.concatenate([zeros_col, shares], axis=1)
    sends = jnp.where(lanes < target, before, jnp.where(lanes == target, SLOT, after))
    return (living, sends.astype(jnp.int32))


def draw_cell_counts(key, part):
    return count_tables(key)[0]


def draw_send_counts(key, part):
    return count_tables(key)[1]


def draw_neighbor_blocks(key, part):
    rows = N_SLAB * N_TILE * NB
    span = NB + 2 * HB
    keys = jax.random.split(jax.random.fold_in(key, 11), rows)
    own = (HB + jnp.arange(rows, dtype=jnp.int32) % NB).astype(jnp.int32)

    def choose(single, itself):
        order = jax.random.permutation(single, span - 1)[:K - 1].astype(jnp.int32)
        order = jnp.where(order >= itself, order + 1, order)
        return jnp.concatenate([itself[None], order])
    return jax.vmap(choose)(keys, own).astype(jnp.int32)


def touch_ends(values, stream_key, least, high):
    shape = values.shape
    index_at = [jax.random.randint(jax.random.fold_in(stream_key, axis), (), 0, shape[axis]) for axis in range(len(shape))]
    values = values.at[tuple(index_at)].set(least)
    longest = shape.index(max(shape))
    index_at[longest] = (index_at[longest] + 1) % shape[longest]
    return values.at[tuple(index_at)].set(high)


def shard_levels(rng, extent, cuts, low, largest):
    factor_of, own = 1.0, jax.random.fold_in(rng, 6)
    for position, shards_of in cuts:
        steps = jnp.exp(jax.random.uniform(jax.random.fold_in(own, position), (shards_of,), jnp.float32, low / len(cuts), largest / len(cuts)))
        factor_of = factor_of * jnp.repeat(steps, extent[position] // shards_of).reshape([-1 if axis == position else 1 for axis in range(len(extent))])
    return factor_of


def scatter_about(key, extent, deviation, bound, cuts=(), kind=jnp.bfloat16):
    gain = shard_levels(key, extent, cuts, -0.22, 0.18) if cuts else 1.0
    drawn = jax.random.normal(key, extent, jnp.float32) * deviation * gain
    return jnp.minimum(jnp.maximum(drawn, -bound), bound).astype(kind)


def setup_inputs(seed: int = 0) -> dict:
    splits = jax.random.split(jax.random.key(seed), 9)
    positions = scatter_about(splits[0], (3, CELLS), 1.0, 6.0, ((1, 32),), jnp.float32)
    radius = jnp.clip(jnp.exp(math.log(1.4) - 0.6931472 * jax.random.uniform(splits[1], (CELLS,), jnp.float32) ** shard_levels(splits[1], (CELLS,), ((0, 32),), -0.2, 0.2)), 0.7, 1.4)
    uptake_rate = jnp.clip(jnp.exp(math.log(3.0) - 2.3025851 * jax.random.uniform(splits[2], (CELLS,), jnp.float32) ** shard_levels(splits[2], (CELLS,), ((0, 32),), -0.2, 0.2)), 0.3, 3.0)
    voxel_local = touch_ends(jax.random.randint(splits[3], (CELLS,), 0, CZ * CY * NX), jax.random.fold_in(splits[3], 1), 0, (CZ * CY * NX) - 1).astype(jnp.int32)
    cell_counts = draw_cell_counts(jax.random.fold_in(splits[8], 71), 0)
    send_counts = draw_send_counts(jax.random.fold_in(splits[8], 71), 0)
    neighbor_blocks = draw_neighbor_blocks(jax.random.fold_in(splits[8], 71), 0)
    field = jnp.clip(0.2 + 1.8 * jax.random.uniform(splits[7], (2, NZ, NY, NX), jnp.float32) ** shard_levels(splits[7], (2, NZ, NY, NX), ((1, 4), (2, 8)), -0.2, 0.2), 0.2, 2.0)
    return dict(positions=positions, radius=radius, uptake_rate=uptake_rate, voxel_local=voxel_local, cell_counts=cell_counts, send_counts=send_counts, neighbor_blocks=neighbor_blocks, field=field)


MICHAELIS_HALF = 0.5
HYPOXIA_HALF = 0.6
SECRETION = 0.4
STEP_TIME = 0.5
DIFFUSION = (0.16, 0.12)
DECAY = (0.0, 0.03)
REPULSION = 1.0
ADHESION = 0.35
REPEL_RANGE = 1.0
ADHERE_RANGE = 4.0
FORCE_SCALE = 0.08
CHEMOTAXIS = 1.5


def block_force(mine, others):
    offset = mine[:3, :, :, None, None] - others[:3, :, None, :, :]
    distance = jnp.sum(offset * offset, axis=0)
    strength = REPULSION * jnp.exp(-distance / REPEL_RANGE) - ADHESION * jnp.exp(-distance / ADHERE_RANGE)
    weight = mine[3][:, :, None, None] * others[3][:, None, :, :] * strength
    return jnp.sum(offset * weight[None], axis=(3, 4))


def relax(padded):
    center = padded[:, 1:-1, 1:-1]
    sideways = jnp.pad(center, ((0, 0), (0, 0), (0, 0), (1, 1)))
    beside_all = padded[:, 2:, 1:-1] + padded[:, :-2, 1:-1]
    beside_all = beside_all + padded[:, 1:-1, 2:] + padded[:, 1:-1, :-2]
    beside_all = beside_all + sideways[..., 2:] + sideways[..., :-2]
    spread = jnp.array(DIFFUSION, jnp.float32)[:, None, None, None]
    losses = jnp.array(DECAY, jnp.float32)[:, None, None, None]
    return center + spread * (beside_all - 6.0 * center) - losses * center


def routing(sends, length):
    ends = jnp.cumsum(sends).astype(jnp.int32)
    starts = (ends - sends).astype(jnp.int32)
    cell = jnp.arange(length, dtype=jnp.int32)
    target = jnp.sum((ends[:, None] <= cell[None, :]).astype(jnp.int32), axis=0).astype(jnp.int32)
    routed = target < sends.shape[0]
    target = jnp.minimum(target, sends.shape[0] - 1).astype(jnp.int32)
    lanes = jnp.arange(sends.shape[0], dtype=jnp.int32)
    first = jnp.sum(jnp.where(lanes[:, None] == target[None, :], starts[:, None], 0), axis=0).astype(jnp.int32)
    return target, (cell - first).astype(jnp.int32), routed


def reference(positions, radius, uptake_rate, voxel_local, cell_counts, send_counts, neighbor_blocks, field):
    devices = N_SLAB * N_TILE
    width = HB * 128
    cell = jnp.arange(CAP, dtype=jnp.int32)
    live = cell[None, :] < cell_counts[:, None]
    kept = jnp.where(live, radius.reshape(devices, CAP), 0.0)
    table = jnp.concatenate([positions.reshape(3, devices, CAP), kept[None]], axis=0)
    grid = table.reshape(4, N_SLAB, N_TILE, CAP)
    blank = jnp.zeros((4, N_SLAB, 1, width), jnp.float32)
    lower = jnp.concatenate([blank, grid[:, :, :-1, CAP - width:]], axis=2)
    upper = jnp.concatenate([grid[:, :, 1:, :width], blank], axis=2)
    extended = jnp.concatenate([lower, grid, upper], axis=3).reshape(4, devices, NB + 2 * HB, 128)
    extended = jnp.moveaxis(extended, 1, 0)
    lists = neighbor_blocks.reshape(devices, NB, K)

    def device_force(pair):
        frame, chosen = pair
        mine = frame[:, HB:HB + NB]
        others = jnp.take(frame, chosen.reshape(-1), axis=1).reshape(4, NB, K, 128)
        return block_force(mine, others)

    forces = lax.map(device_force, (extended, lists))
    forces = jnp.moveaxis(forces, 1, 0).reshape(3, devices * CAP)

    target, rank, routed = jax.vmap(lambda sends: routing(sends, CAP))(send_counts)
    slab_of = jnp.broadcast_to((jnp.arange(devices, dtype=jnp.int32) // N_TILE)[:, None], (devices, CAP))
    voxels = voxel_local.reshape(devices, CAP)
    volume = CZ * CY * NX
    blocks = field.reshape(2, N_SLAB, CZ, N_TILE, CY, NX).transpose(1, 3, 0, 2, 4, 5).reshape(N_SLAB, N_TILE, 2, volume)
    oxygen = blocks[slab_of, target, 0, voxels]
    rates = jnp.where(routed, uptake_rate.reshape(devices, CAP), 0.0)
    consume = rates * oxygen / (MICHAELIS_HALF + oxygen)
    secrete = SECRETION * rates * HYPOXIA_HALF / (HYPOXIA_HALF + oxygen)
    blocks = blocks.at[slab_of, target, 0, voxels].add(-STEP_TIME * consume)
    blocks = blocks.at[slab_of, target, 1, voxels].add(STEP_TIME * secrete)
    state = blocks.reshape(N_SLAB, N_TILE, 2, CZ, CY, NX).transpose(2, 0, 3, 1, 4, 5).reshape(2, N_SLAB * CZ, N_TILE * CY, NX)
    for step in range(ITERS):
        state = relax(jnp.pad(state, ((0, 0), (1, 1), (1, 1), (0, 0))))

    vegf = jnp.pad(state[1], 1)
    depth_at = slab_of * CZ + voxels // (CY * NX) + 1
    row_at = target * CY + (voxels // NX) % CY + 1
    column_at = voxels % NX + 1
    rise_z = 0.5 * (vegf[depth_at + 1, row_at, column_at] - vegf[depth_at - 1, row_at, column_at])
    rise_y = 0.5 * (vegf[depth_at, row_at + 1, column_at] - vegf[depth_at, row_at - 1, column_at])
    rise_x = 0.5 * (vegf[depth_at, row_at, column_at + 1] - vegf[depth_at, row_at, column_at - 1])
    slope = jnp.where(routed[None], jnp.stack([rise_z, rise_y, rise_x]), 0.0).reshape(3, devices * CAP)
    velocity = FORCE_SCALE * forces + CHEMOTAXIS * slope
    return velocity, state
```

```python
import functools

import jax
import jax.numpy as jnp
from jax import lax
from jax.experimental import pallas as pl
from jax.experimental.pallas import tpu as pltpu
from jax.sharding import PartitionSpec as P

HB = 4
K = 8
ITERS = 4

MICHAELIS_HALF = 0.5
HYPOXIA_HALF = 0.6
SECRETION = 0.4
STEP_TIME = 0.5
DIFFUSION = (0.16, 0.12)
DECAY = (0.0, 0.03)
REPULSION = 1.0
ADHESION = 0.35
FORCE_SCALE = 0.08
CHEMOTAXIS = 1.5

VMEM = pl.BlockSpec(memory_space=pltpu.VMEM)
SMEM = pl.BlockSpec(memory_space=pltpu.SMEM)
LIMIT = pltpu.CompilerParams(vmem_limit_bytes=48 * 1024 * 1024)


def neighbours(block, axis, dim, width):
    count = lax.axis_size(axis)
    forward = [(i, i + 1) for i in range(count - 1)]
    backward = [(target, source) for source, target in forward]
    low = lax.ppermute(
        lax.slice_in_dim(block, block.shape[dim] - width, None, axis=dim), axis, forward
    )
    high = lax.ppermute(lax.slice_in_dim(block, 0, width, axis=dim), axis, backward)
    return low, high


def hot(index, length):
    return lax.broadcasted_iota(jnp.int32, (length, index.shape[1]), 0) == index


def halves(values):
    high = values.astype(jnp.bfloat16)
    low = (values - high.astype(jnp.float32)).astype(jnp.bfloat16)
    return high, low


def dot(a, b, contract):
    return lax.dot_general(
        a, b, ((contract[:1], contract[1:]), ((), ())), preferred_element_type=jnp.float32
    )


def pack_kernel(tiles, slot, sends, cells, out):
    width = slot + 128
    lane = lax.broadcasted_iota(jnp.int32, (2, slot), 1)
    start = jnp.int32(0)
    for d in range(tiles):
        n = sends[0, d]
        base = pl.multiple_of((start >> 7) << 7, 128)
        window = cells[:, pl.ds(base, width)]
        moved = pltpu.roll(window, width - (start - base), 1)
        out[d] = jnp.where(lane < n, moved[:2, :slot], 0.0)
        start = start + n


def unpack_kernel(tiles, slot, sends, back, force, out, padded, total):
    width = slot + 128
    capacity = out.shape[1]
    padded[...] = jnp.zeros_like(padded)
    total[...] = jnp.zeros_like(total)
    lane = lax.broadcasted_iota(jnp.int32, (8, width), 1)
    start = jnp.int32(0)
    for d in range(tiles):
        n = sends[0, d]
        base = pl.multiple_of((start >> 7) << 7, 128)
        shift = start - base
        padded[0:3, 0:slot] = back[d]
        moved = pltpu.roll(padded[...], shift, 1)
        there = jnp.logical_and(lane >= shift, lane < shift + n)
        total[:, pl.ds(base, width)] += jnp.where(there, moved, 0.0)
        start = start + n
    out[...] = FORCE_SCALE * force[0:3] + CHEMOTAXIS * total[0:3, 0:capacity]


def force_kernel(chosen, table, out, wide):
    extended = table.shape[0]

    def spread(e, carry):
        turned = jnp.transpose(table[e])
        for c in range(4):
            wide[e, c] = jnp.broadcast_to(turned[:, c : c + 1], (128, 128))
        return carry

    lax.fori_loop(0, extended, spread, 0)

    def one_block(b, carry):
        mine = table[b + HB]
        at = [jnp.broadcast_to(mine[c : c + 1], (8, 128)) for c in range(3)]

        def one_neighbour(k, sums):
            e = chosen[b, k]
            sx, sy, sz = sums
            for g in range(16):
                rows = slice(8 * g, 8 * g + 8)
                dx = at[0] - wide[e, 0, rows]
                dy = at[1] - wide[e, 1, rows]
                dz = at[2] - wide[e, 2, rows]
                far = jnp.exp(-0.25 * (dx * dx + dy * dy + dz * dz))
                square = far * far
                w = wide[e, 3, rows] * (REPULSION * (square * square) - ADHESION * far)
                sx = sx + w * dx
                sy = sy + w * dy
                sz = sz + w * dz
            return sx, sy, sz

        zero = jnp.zeros((8, 128), jnp.float32)
        sums = lax.fori_loop(0, K, one_neighbour, (zero, zero, zero))
        columns = pl.ds(pl.multiple_of(b * 128, 128), 128)
        for c in range(3):
            out[c : c + 1, columns] = mine[3:4] * jnp.sum(sums[c], axis=0, keepdims=True)
        return carry

    lax.fori_loop(0, out.shape[1] // 128, one_block, 0)


def deposit_kernel(got, field, out, oxygen):
    tiles = got.shape[0]
    planes, columns = field.shape[1:]
    out[...] = field[...]
    high, low = halves(field[0])
    oxygen[0:planes] = high
    oxygen[planes:] = low

    def one_source(t, carry):
        wanted = got[t, 0:1].astype(jnp.int32)
        given = got[t, 1:2]
        row_hot = hot(wanted // columns, planes)
        column_hot = hot(wanted % columns, columns).astype(jnp.bfloat16)
        picked = dot(oxygen[...], column_hot, (1, 0))
        picked = picked[:planes] + picked[planes:]
        o = jnp.sum(jnp.where(row_hot, picked, 0.0), axis=0, keepdims=True)
        consume = given * o / (MICHAELIS_HALF + o)
        secrete = SECRETION * given * HYPOXIA_HALF / (HYPOXIA_HALF + o)
        for s, amount in enumerate((-STEP_TIME * consume, STEP_TIME * secrete)):
            high, low = halves(jnp.where(row_hot, amount, 0.0))
            out[s] += dot(high, column_hot, (1, 1)) + dot(low, column_hot, (1, 1))
        return carry

    lax.fori_loop(0, tiles, one_source, 0)


def slope_kernel(depth, rows, got, vegf, z_low, z_high, y_low, y_high, out, near):
    tiles = got.shape[0]
    planes, columns = vegf.shape
    count = planes + 2 * rows + 2 * depth
    first = 0
    for part in (z_low, vegf, z_high, y_low, y_high):
        high, low = halves(part[...])
        near[first : first + part.shape[0]] = high
        near[count + first : count + first + part.shape[0]] = low
        first += part.shape[0]

    def one_source(t, carry):
        wanted = got[t, 0:1].astype(jnp.int32)
        row, column = wanted // columns, wanted % columns
        z, y = row // rows, row % rows
        inner = hot(column, columns).astype(jnp.bfloat16)
        values = dot(near[...], inner, (1, 0))
        values = values[:count] + values[count:]

        def at(index):
            return jnp.sum(jnp.where(hot(index, count), values, 0.0), axis=0, keepdims=True)

        below = jnp.where(y == 0, planes + 2 * rows + z, row + rows - 1)
        above = jnp.where(y == rows - 1, planes + 2 * rows + depth + z, row + rows + 1)
        out[t, 0:1] = 0.5 * (at(row + 2 * rows) - at(row))
        out[t, 1:2] = 0.5 * (at(above) - at(below))
        right = jnp.where(hot(column + 1, columns), 1.0, 0.0)
        beside = jnp.where(hot(column - 1, columns), -1.0, right).astype(jnp.bfloat16)
        change = dot(near[rows : rows + planes], beside, (1, 0))
        change = change + dot(near[count + rows : count + rows + planes], beside, (1, 0))
        change = jnp.where(hot(row, planes), change, 0.0)
        out[t, 2:3] = 0.5 * jnp.sum(change, axis=0, keepdims=True)
        return carry

    lax.fori_loop(0, tiles, one_source, 0)


def relax(center, z_low, z_high, y_low, y_high):
    along_z = jnp.concatenate([z_low, center, z_high], axis=1)
    along_y = jnp.concatenate([y_low, center, y_high], axis=2)
    along_x = jnp.pad(center, ((0, 0), (0, 0), (0, 0), (1, 1)))
    around = along_z[:, 2:] + along_z[:, :-2] + along_y[:, :, 2:] + along_y[:, :, :-2]
    around = around + along_x[..., 2:] + along_x[..., :-2]
    spread = jnp.array(DIFFUSION, jnp.float32)[:, None, None, None]
    losses = jnp.array(DECAY, jnp.float32)[:, None, None, None]
    return center + spread * (around - 6.0 * center) - losses * center


def shape_of(*shape):
    return jax.ShapeDtypeStruct(shape, jnp.float32)


def local(
    positions, radius, uptake_rate, voxel_local, cell_counts, send_counts, neighbor_blocks, field
):
    tiles = lax.axis_size("tile")
    capacity = positions.shape[1]
    slot = 2 * capacity // tiles
    blocks = capacity // 128
    species, depth, rows, columns = field.shape
    planes = depth * rows

    cells = jnp.stack([voxel_local.astype(jnp.float32), uptake_rate])
    cells = jnp.pad(cells, ((0, 6), (0, slot + 128)))
    packed = pl.pallas_call(
        functools.partial(pack_kernel, tiles, slot),
        out_shape=shape_of(tiles, 2, slot),
        in_specs=[SMEM, VMEM],
        out_specs=VMEM,
        compiler_params=LIMIT,
    )(send_counts, cells)
    got = lax.all_to_all(packed, "tile", split_axis=0, concat_axis=0, tiled=True)

    cell = jnp.arange(capacity, dtype=jnp.int32)
    kept = jnp.where(cell < cell_counts[0], radius, 0.0)
    table = jnp.concatenate([positions, kept[None]], axis=0)
    low, high = neighbours(table, "tile", 1, HB * 128)
    extended = jnp.concatenate([low, table, high], axis=1)
    extended = extended.reshape(4, blocks + 2 * HB, 128).transpose(1, 0, 2)
    extended = jnp.pad(extended, ((0, 0), (0, 4), (0, 0)))
    force = pl.pallas_call(
        force_kernel,
        out_shape=shape_of(8, capacity),
        in_specs=[SMEM, VMEM],
        out_specs=VMEM,
        scratch_shapes=[pltpu.VMEM((blocks + 2 * HB, 4, 128, 128), jnp.float32)],
        compiler_params=LIMIT,
        cost_estimate=pl.CostEstimate(
            flops=20 * capacity * K * 128, bytes_accessed=1 << 19, transcendentals=capacity * K * 128
        ),
    )(neighbor_blocks, extended)

    state = pl.pallas_call(
        deposit_kernel,
        out_shape=shape_of(species, planes, columns),
        in_specs=[VMEM, VMEM],
        out_specs=VMEM,
        scratch_shapes=[pltpu.VMEM((2 * planes, columns), jnp.bfloat16)],
        compiler_params=LIMIT,
    )(got, field.reshape(species, planes, columns))
    state = state.reshape(field.shape)
    for step in range(ITERS):
        state = relax(state, *neighbours(state, "slab", 1, 1), *neighbours(state, "tile", 2, 1))

    vegf = state[1]
    z_low, z_high = neighbours(vegf, "slab", 0, 1)
    y_low, y_high = neighbours(vegf, "tile", 1, 1)
    slopes = pl.pallas_call(
        functools.partial(slope_kernel, depth, rows),
        out_shape=shape_of(tiles, 3, slot),
        in_specs=[VMEM] * 6,
        out_specs=VMEM,
        scratch_shapes=[
            pltpu.VMEM((2 * (planes + 2 * rows + 2 * depth), columns), jnp.bfloat16)
        ],
        compiler_params=LIMIT,
    )(
        got,
        vegf.reshape(planes, columns),
        z_low.reshape(rows, columns),
        z_high.reshape(rows, columns),
        y_low.reshape(depth, columns),
        y_high.reshape(depth, columns),
    )
    back = lax.all_to_all(slopes, "tile", split_axis=0, concat_axis=0, tiled=True)
    velocity = pl.pallas_call(
        functools.partial(unpack_kernel, tiles, slot),
        out_shape=shape_of(3, capacity),
        in_specs=[SMEM, VMEM, VMEM],
        out_specs=VMEM,
        scratch_shapes=[
            pltpu.VMEM((8, slot + 128), jnp.float32),
            pltpu.VMEM((8, capacity + slot + 128), jnp.float32),
        ],
        compiler_params=LIMIT,
    )(send_counts, back, force)
    return (velocity, state)


def solution(mesh):
    placed = (
        P(None, ("slab", "tile")),
        P(("slab", "tile")),
        P(("slab", "tile")),
        P(("slab", "tile")),
        P(("slab", "tile")),
        P(("slab", "tile"), None),
        P(("slab", "tile"), None),
        P(None, "slab", "tile", None),
    )
    return jax.shard_map(
        local,
        mesh=mesh,
        in_specs=placed,
        out_specs=(P(None, ("slab", "tile")), P(None, "slab", "tile", None)),
        check_vma=False,
    )
```

```python
import functools

import jax
import jax.numpy as jnp
from jax import lax
from jax.experimental import pallas as pl
from jax.experimental.pallas import tpu as pltpu
from jax.sharding import PartitionSpec as P

HB = 4
K = 8
ITERS = 4

MICHAELIS_HALF = 0.5
HYPOXIA_HALF = 0.6
SECRETION = 0.4
STEP_TIME = 0.5
DIFFUSION = (0.16, 0.12)
DECAY = (0.0, 0.03)
REPULSION = 1.0
ADHESION = 0.35
FORCE_SCALE = 0.08
CHEMOTAXIS = 1.5

VMEM = pl.BlockSpec(memory_space=pltpu.VMEM)
SMEM = pl.BlockSpec(memory_space=pltpu.SMEM)
LIMIT = pltpu.CompilerParams(vmem_limit_bytes=48 * 1024 * 1024)


MESH = pl.DeviceIdType.MESH


def swap(tiles, source, held, send_sem, recv_sem):
    me = lax.axis_index("tile")
    copies = []
    for i in range(1, tiles):
        to = lax.rem(me + i, tiles)
        copy = pltpu.make_async_remote_copy(
            src_ref=source.at[to],
            dst_ref=held.at[me],
            send_sem=send_sem.at[i],
            recv_sem=recv_sem.at[i],
            device_id={"tile": to},
            device_id_type=MESH,
        )
        copy.start()
        copies.append(copy)
    return copies


def greet(tiles):
    me = lax.axis_index("tile")
    barrier = pltpu.get_barrier_semaphore()
    for i in range(1, tiles):
        pl.semaphore_signal(
            barrier, inc=1, device_id={"tile": lax.rem(me + i, tiles)}, device_id_type=MESH
        )
    pl.semaphore_wait(barrier, tiles - 1)


def meet_kernel(tiles, packed, table, got, extended, held, sides, send_sem, recv_sem, side_sem):
    me = lax.axis_index("tile")
    capacity = table.shape[1]
    width = HB * 128
    sides[...] = jnp.zeros_like(sides)
    greet(tiles)
    copies = swap(tiles, packed, held, send_sem, recv_sem)
    up = pltpu.make_async_remote_copy(
        src_ref=table.at[:, capacity - width :],
        dst_ref=sides.at[0],
        send_sem=side_sem.at[0],
        recv_sem=side_sem.at[1],
        device_id={"tile": jnp.minimum(me + 1, tiles - 1)},
        device_id_type=MESH,
    )
    down = pltpu.make_async_remote_copy(
        src_ref=table.at[:, :width],
        dst_ref=sides.at[1],
        send_sem=side_sem.at[2],
        recv_sem=side_sem.at[3],
        device_id={"tile": jnp.maximum(me - 1, 0)},
        device_id_type=MESH,
    )

    @pl.when(me < tiles - 1)
    def _():
        up.start()

    @pl.when(me > 0)
    def _():
        down.start()

    blocks = capacity // 128
    extended[...] = jnp.zeros_like(extended)
    for b in range(blocks):
        extended[HB + b, 0:4] = table[:, 128 * b : 128 * b + 128]
    got[me] = packed[me]

    @pl.when(me < tiles - 1)
    def _():
        up.wait_send()
        down.wait_recv()

    @pl.when(me > 0)
    def _():
        down.wait_send()
        up.wait_recv()

    for b in range(HB):
        extended[b, 0:4] = sides[0, :, 128 * b : 128 * b + 128]
        extended[HB + blocks + b, 0:4] = sides[1, :, 128 * b : 128 * b + 128]
    for copy in copies:
        copy.wait()
    for i in range(1, tiles):
        other = lax.rem(me + i, tiles)
        got[other] = held[other]


def return_kernel(tiles, slopes, back, held, send_sem, recv_sem):
    me = lax.axis_index("tile")
    greet(tiles)
    copies = swap(tiles, slopes, held, send_sem, recv_sem)
    back[me] = slopes[me]
    for copy in copies:
        copy.wait()
    for i in range(1, tiles):
        other = lax.rem(me + i, tiles)
        back[other] = held[other]


def hot(index, length):
    return lax.broadcasted_iota(jnp.int32, (length, index.shape[1]), 0) == index


def halves(values):
    high = values.astype(jnp.bfloat16)
    low = (values - high.astype(jnp.float32)).astype(jnp.bfloat16)
    return high, low


def dot(a, b, contract):
    return lax.dot_general(
        a, b, ((contract[:1], contract[1:]), ((), ())), preferred_element_type=jnp.float32
    )


def pack_kernel(tiles, slot, sends, cells, out):
    width = slot + 128
    lane = lax.broadcasted_iota(jnp.int32, (2, slot), 1)
    start = jnp.int32(0)
    for d in range(tiles):
        n = sends[0, d]
        base = pl.multiple_of((start >> 7) << 7, 128)
        window = cells[:, pl.ds(base, width)]
        moved = pltpu.roll(window, width - (start - base), 1)
        out[d] = jnp.where(lane < n, moved[:2, :slot], 0.0)
        start = start + n


def unpack_kernel(tiles, slot, sends, back, force, out, padded, total):
    width = slot + 128
    capacity = out.shape[1]
    padded[...] = jnp.zeros_like(padded)
    total[...] = jnp.zeros_like(total)
    lane = lax.broadcasted_iota(jnp.int32, (8, width), 1)
    start = jnp.int32(0)
    for d in range(tiles):
        n = sends[0, d]
        base = pl.multiple_of((start >> 7) << 7, 128)
        shift = start - base
        padded[0:3, 0:slot] = back[d]
        moved = pltpu.roll(padded[...], shift, 1)
        there = jnp.logical_and(lane >= shift, lane < shift + n)
        total[:, pl.ds(base, width)] += jnp.where(there, moved, 0.0)
        start = start + n
    out[...] = FORCE_SCALE * force[0:3] + CHEMOTAXIS * total[0:3, 0:capacity]


def widen(table, wide):
    def one(e, carry):
        turned = jnp.transpose(table[e])
        for c in range(4):
            wide[e, c] = jnp.broadcast_to(turned[:, c : c + 1], (128, 128))
        return carry

    lax.fori_loop(0, table.shape[0], one, 0)


def force_blocks(chosen, table, wide, out, first, last):
    def one_block(b, carry):
        mine = table[b + HB]
        at = [jnp.broadcast_to(mine[c : c + 1], (8, 128)) for c in range(3)]

        def one_neighbour(k, sums):
            e = chosen[b, k]
            sx, sy, sz = sums
            for g in range(16):
                rows = slice(8 * g, 8 * g + 8)
                dx = at[0] - wide[e, 0, rows]
                dy = at[1] - wide[e, 1, rows]
                dz = at[2] - wide[e, 2, rows]
                far = jnp.exp(-0.25 * (dx * dx + dy * dy + dz * dz))
                square = far * far
                w = wide[e, 3, rows] * (REPULSION * (square * square) - ADHESION * far)
                sx = sx + w * dx
                sy = sy + w * dy
                sz = sz + w * dz
            return sx, sy, sz

        zero = jnp.zeros((8, 128), jnp.float32)
        sums = lax.fori_loop(0, K, one_neighbour, (zero, zero, zero))
        columns = pl.ds(pl.multiple_of(b * 128, 128), 128)
        for c in range(3):
            out[c : c + 1, columns] = mine[3:4] * jnp.sum(sums[c], axis=0, keepdims=True)
        return carry

    lax.fori_loop(first, last, one_block, 0)


def diffuse_kernel(
    slabs,
    tiles,
    chosen,
    table,
    start,
    out,
    force,
    edge_z,
    edge_y,
    state,
    wide,
    sent_y,
    halo_z,
    halo_y,
    send_sem,
    recv_sem,
):
    species, depth, rows, columns = start.shape
    slab, tile = lax.axis_index("slab"), lax.axis_index("tile")
    sides = (
        ("slab", slab, slabs, 0),
        ("slab", slab, slabs, 1),
        ("tile", tile, tiles, 0),
        ("tile", tile, tiles, 1),
    )

    def exists(side):
        axis, at, count, up = side
        return at < count - 1 if up else at > 0

    def partner(side):
        axis, at, count, up = side
        return {axis: jnp.minimum(at + 1, count - 1) if up else jnp.maximum(at - 1, 0)}

    halo_z[...] = jnp.zeros_like(halo_z)
    halo_y[...] = jnp.zeros_like(halo_y)
    barrier = pltpu.get_barrier_semaphore()
    for side in sides:

        @pl.when(exists(side))
        def _(side=side):
            pl.semaphore_signal(barrier, inc=1, device_id=partner(side), device_id_type=MESH)

    count = sum(exists(side).astype(jnp.int32) for side in sides)
    pl.semaphore_wait(barrier, count)

    def copies(step, now, which):
        made = []
        for n, side in enumerate(sides):
            up = side[3]
            if n < 2:
                source = state.at[now, which, depth if up else 1]
                target = halo_z.at[step, 1 - up, which]
            else:
                source = sent_y.at[step, up, which]
                target = halo_y.at[step, 1 - up, which]
            made.append(
                pltpu.make_async_remote_copy(
                    src_ref=source,
                    dst_ref=target,
                    send_sem=send_sem.at[step, n],
                    recv_sem=recv_sem.at[step, n],
                    device_id=partner(side),
                    device_id_type=MESH,
                )
            )
        return made

    def begin(step, now, which):
        for up in range(2):
            sent_y[step, up] = state[now, :, 1 : depth + 1, (rows - 1) * up, :]
        made = copies(step, now, which)
        for n in (2, 3, 0, 1):

            @pl.when(exists(sides[n]))
            def _(n=n):
                made[n].start()

        return made

    def finish(made):
        for n, side in enumerate(sides):

            @pl.when(exists(side))
            def _(n=n):
                made[n].wait_send()
                made[n ^ 1].wait_recv()

    blocks = force.shape[1] // 128
    share = blocks // (ITERS + 1)
    for now in range(2):
        for s in range(species):
            for z in (0, depth + 1):
                state[now, s, z] = jnp.zeros((rows, columns), jnp.float32)
    state[0, :, 1 : depth + 1] = start[...]
    lane = lax.broadcasted_iota(jnp.int32, (rows, columns), 1)
    row = lax.broadcasted_iota(jnp.int32, (rows, columns), 0)

    def one_step(step, carry):
        now = lax.rem(step, 2)
        later = 1 - now
        made = begin(step, now, slice(0, species))

        @pl.when(step == 0)
        def _():
            widen(table, wide)

        for s in range(species):

            def one_plane(z, carry):
                c = state[now, s, z]
                around = state[now, s, z - 1] + state[now, s, z + 1]
                around += jnp.where(row == 0, 0.0, pltpu.roll(c, 1, 0))
                around += jnp.where(row == rows - 1, 0.0, pltpu.roll(c, rows - 1, 0))
                around += jnp.where(lane == 0, 0.0, pltpu.roll(c, 1, 1))
                around += jnp.where(lane == columns - 1, 0.0, pltpu.roll(c, columns - 1, 1))
                state[later, s, z] = c + DIFFUSION[s] * (around - 6.0 * c) - DECAY[s] * c
                return carry

            lax.fori_loop(1, depth + 1, one_plane, 0)
        force_blocks(chosen, table, wide, force, step * share, (step + 1) * share)
        finish(made)
        for s in range(species):
            for up in range(2):
                state[later, s, depth if up else 1] += DIFFUSION[s] * halo_z[step, up, s]
                for z in range(depth):
                    edge = slice((rows - 1) * up, (rows - 1) * up + 1)
                    state[later, s, z + 1, edge] += DIFFUSION[s] * halo_y[step, up, s, z : z + 1]
        return carry

    lax.fori_loop(0, ITERS, one_step, 0)
    last = ITERS % 2
    made = begin(ITERS, last, 1)
    force_blocks(chosen, table, wide, force, ITERS * share, blocks)
    out[...] = state[last, :, 1 : depth + 1]
    finish(made)
    edge_z[...] = halo_z[ITERS, :, 1]
    edge_y[...] = halo_y[ITERS, :, 1]


def deposit_kernel(got, field, out, oxygen):
    tiles = got.shape[0]
    planes, columns = field.shape[1:]
    out[...] = field[...]
    high, low = halves(field[0])
    oxygen[0:planes] = high
    oxygen[planes:] = low

    def one_source(t, carry):
        wanted = got[t, 0:1].astype(jnp.int32)
        given = got[t, 1:2]
        row_hot = hot(wanted // columns, planes)
        column_hot = hot(wanted % columns, columns).astype(jnp.bfloat16)
        picked = dot(oxygen[...], column_hot, (1, 0))
        picked = picked[:planes] + picked[planes:]
        o = jnp.sum(jnp.where(row_hot, picked, 0.0), axis=0, keepdims=True)
        consume = given * o / (MICHAELIS_HALF + o)
        secrete = SECRETION * given * HYPOXIA_HALF / (HYPOXIA_HALF + o)
        for s, amount in enumerate((-STEP_TIME * consume, STEP_TIME * secrete)):
            high, low = halves(jnp.where(row_hot, amount, 0.0))
            out[s] += dot(high, column_hot, (1, 1)) + dot(low, column_hot, (1, 1))
        return carry

    lax.fori_loop(0, tiles, one_source, 0)


def slope_kernel(depth, rows, got, field, edge_z, edge_y, out, near):
    tiles = got.shape[0]
    planes, columns = field.shape[1:]
    count = planes + 2 * rows + 2 * depth
    first = 0
    for part in (edge_z[0], field[1], edge_z[1], edge_y[0], edge_y[1]):
        high, low = halves(part)
        near[first : first + part.shape[0]] = high
        near[count + first : count + first + part.shape[0]] = low
        first += part.shape[0]

    def one_source(t, carry):
        wanted = got[t, 0:1].astype(jnp.int32)
        row, column = wanted // columns, wanted % columns
        z, y = row // rows, row % rows
        inner = hot(column, columns).astype(jnp.bfloat16)
        values = dot(near[...], inner, (1, 0))
        values = values[:count] + values[count:]

        def at(index):
            return jnp.sum(jnp.where(hot(index, count), values, 0.0), axis=0, keepdims=True)

        below = jnp.where(y == 0, planes + 2 * rows + z, row + rows - 1)
        above = jnp.where(y == rows - 1, planes + 2 * rows + depth + z, row + rows + 1)
        out[t, 0:1] = 0.5 * (at(row + 2 * rows) - at(row))
        out[t, 1:2] = 0.5 * (at(above) - at(below))
        right = jnp.where(hot(column + 1, columns), 1.0, 0.0)
        beside = jnp.where(hot(column - 1, columns), -1.0, right).astype(jnp.bfloat16)
        change = dot(near[rows : rows + planes], beside, (1, 0))
        change = change + dot(near[count + rows : count + rows + planes], beside, (1, 0))
        change = jnp.where(hot(row, planes), change, 0.0)
        out[t, 2:3] = 0.5 * jnp.sum(change, axis=0, keepdims=True)
        return carry

    lax.fori_loop(0, tiles, one_source, 0)


def remote(number):
    return pltpu.CompilerParams(
        vmem_limit_bytes=48 * 1024 * 1024, collective_id=number, has_side_effects=True
    )


def shape_of(*shape):
    return jax.ShapeDtypeStruct(shape, jnp.float32)


def local(
    positions, radius, uptake_rate, voxel_local, cell_counts, send_counts, neighbor_blocks, field
):
    slabs, tiles = lax.axis_size("slab"), lax.axis_size("tile")
    capacity = positions.shape[1]
    slot = 2 * capacity // tiles
    blocks = capacity // 128
    species, depth, rows, columns = field.shape
    planes = depth * rows

    cells = jnp.stack([voxel_local.astype(jnp.float32), uptake_rate])
    cells = jnp.pad(cells, ((0, 6), (0, slot + 128)))
    packed = pl.pallas_call(
        functools.partial(pack_kernel, tiles, slot),
        out_shape=shape_of(tiles, 2, slot),
        in_specs=[SMEM, VMEM],
        out_specs=VMEM,
        compiler_params=LIMIT,
    )(send_counts, cells)
    cell = jnp.arange(capacity, dtype=jnp.int32)
    kept = jnp.where(cell < cell_counts[0], radius, 0.0)
    table = jnp.concatenate([positions, kept[None]], axis=0)
    got, extended = pl.pallas_call(
        functools.partial(meet_kernel, tiles),
        out_shape=(shape_of(tiles, 2, slot), shape_of(blocks + 2 * HB, 8, 128)),
        in_specs=[VMEM, VMEM],
        out_specs=[VMEM, VMEM],
        scratch_shapes=[
            pltpu.VMEM((tiles, 2, slot), jnp.float32),
            pltpu.VMEM((2, 4, HB * 128), jnp.float32),
            pltpu.SemaphoreType.DMA((tiles,)),
            pltpu.SemaphoreType.DMA((tiles,)),
            pltpu.SemaphoreType.DMA((4,)),
        ],
        compiler_params=remote(0),
    )(packed, table)

    state = pl.pallas_call(
        deposit_kernel,
        out_shape=shape_of(species, planes, columns),
        in_specs=[VMEM, VMEM],
        out_specs=VMEM,
        scratch_shapes=[pltpu.VMEM((2 * planes, columns), jnp.bfloat16)],
        compiler_params=LIMIT,
    )(got, field.reshape(species, planes, columns))
    steps = ITERS + 1
    state, force, edge_z, edge_y = pl.pallas_call(
        functools.partial(diffuse_kernel, slabs, tiles),
        out_shape=(
            shape_of(*field.shape),
            shape_of(8, capacity),
            shape_of(2, rows, columns),
            shape_of(2, depth, columns),
        ),
        in_specs=[SMEM, VMEM, VMEM],
        out_specs=[VMEM] * 4,
        scratch_shapes=[
            pltpu.VMEM((2, species, depth + 2, rows, columns), jnp.float32),
            pltpu.VMEM((blocks + 2 * HB, 4, 128, 128), jnp.float32),
            pltpu.VMEM((steps, 2, species, depth, columns), jnp.float32),
            pltpu.VMEM((steps, 2, species, rows, columns), jnp.float32),
            pltpu.VMEM((steps, 2, species, depth, columns), jnp.float32),
            pltpu.SemaphoreType.DMA((steps, 4)),
            pltpu.SemaphoreType.DMA((steps, 4)),
        ],
        compiler_params=remote(1),
    )(neighbor_blocks, extended, state.reshape(field.shape))

    slopes = pl.pallas_call(
        functools.partial(slope_kernel, depth, rows),
        out_shape=shape_of(tiles, 3, slot),
        in_specs=[VMEM] * 4,
        out_specs=VMEM,
        scratch_shapes=[
            pltpu.VMEM((2 * (planes + 2 * rows + 2 * depth), columns), jnp.bfloat16)
        ],
        compiler_params=LIMIT,
    )(got, state.reshape(species, planes, columns), edge_z, edge_y)
    back = pl.pallas_call(
        functools.partial(return_kernel, tiles),
        out_shape=shape_of(tiles, 3, slot),
        in_specs=[VMEM],
        out_specs=VMEM,
        scratch_shapes=[
            pltpu.VMEM((tiles, 3, slot), jnp.float32),
            pltpu.SemaphoreType.DMA((tiles,)),
            pltpu.SemaphoreType.DMA((tiles,)),
        ],
        compiler_params=remote(2),
    )(slopes)
    velocity = pl.pallas_call(
        functools.partial(unpack_kernel, tiles, slot),
        out_shape=shape_of(3, capacity),
        in_specs=[SMEM, VMEM, VMEM],
        out_specs=VMEM,
        scratch_shapes=[
            pltpu.VMEM((8, slot + 128), jnp.float32),
            pltpu.VMEM((8, capacity + slot + 128), jnp.float32),
        ],
        compiler_params=LIMIT,
    )(send_counts, back, force)
    return (velocity, state)


def solution(mesh):
    placed = (
        P(None, ("slab", "tile")),
        P(("slab", "tile")),
        P(("slab", "tile")),
        P(("slab", "tile")),
        P(("slab", "tile")),
        P(("slab", "tile"), None),
        P(("slab", "tile"), None),
        P(None, "slab", "tile", None),
    )
    return jax.shard_map(
        local,
        mesh=mesh,
        in_specs=placed,
        out_specs=(P(None, ("slab", "tile")), P(None, "slab", "tile", None)),
        check_vma=False,
    )
```

```python
import functools

import jax
import jax.numpy as jnp
from jax import lax
from jax.experimental import pallas as pl
from jax.experimental.pallas import tpu as pltpu
from jax.sharding import PartitionSpec as P

HB = 4
K = 8
ITERS = 4

MICHAELIS_HALF = 0.5
HYPOXIA_HALF = 0.6
SECRETION = 0.4
STEP_TIME = 0.5
DIFFUSION = (0.16, 0.12)
DECAY = (0.0, 0.03)
REPULSION = 1.0
ADHESION = 0.35
FORCE_SCALE = 0.08
CHEMOTAXIS = 1.5

VMEM = pl.BlockSpec(memory_space=pltpu.VMEM)
SMEM = pl.BlockSpec(memory_space=pltpu.SMEM)
LIMIT = pltpu.CompilerParams(vmem_limit_bytes=48 * 1024 * 1024)


MESH = pl.DeviceIdType.MESH


def swap(tiles, source, held, send_sem, recv_sem):
    me = lax.axis_index("tile")
    copies = []
    for i in range(1, tiles):
        to = lax.rem(me + i, tiles)
        copy = pltpu.make_async_remote_copy(
            src_ref=source.at[to],
            dst_ref=held.at[me],
            send_sem=send_sem.at[i],
            recv_sem=recv_sem.at[i],
            device_id={"tile": to},
            device_id_type=MESH,
        )
        copy.start()
        copies.append(copy)
    return copies


def greet(tiles):
    me = lax.axis_index("tile")
    barrier = pltpu.get_barrier_semaphore()
    for i in range(1, tiles):
        pl.semaphore_signal(
            barrier, inc=1, device_id={"tile": lax.rem(me + i, tiles)}, device_id_type=MESH
        )
    pl.semaphore_wait(barrier, tiles - 1)


def meet_kernel(tiles, packed, table, got, extended, held, sides, send_sem, recv_sem, side_sem):
    me = lax.axis_index("tile")
    capacity = table.shape[1]
    width = HB * 128
    sides[...] = jnp.zeros_like(sides)
    greet(tiles)
    copies = swap(tiles, packed, held, send_sem, recv_sem)
    up = pltpu.make_async_remote_copy(
        src_ref=table.at[:, capacity - width :],
        dst_ref=sides.at[0],
        send_sem=side_sem.at[0],
        recv_sem=side_sem.at[1],
        device_id={"tile": jnp.minimum(me + 1, tiles - 1)},
        device_id_type=MESH,
    )
    down = pltpu.make_async_remote_copy(
        src_ref=table.at[:, :width],
        dst_ref=sides.at[1],
        send_sem=side_sem.at[2],
        recv_sem=side_sem.at[3],
        device_id={"tile": jnp.maximum(me - 1, 0)},
        device_id_type=MESH,
    )

    @pl.when(me < tiles - 1)
    def _():
        up.start()

    @pl.when(me > 0)
    def _():
        down.start()

    blocks = capacity // 128
    extended[...] = jnp.zeros_like(extended)
    for b in range(blocks):
        extended[HB + b, 0:4] = table[:, 128 * b : 128 * b + 128]
    got[me] = packed[me]

    @pl.when(me < tiles - 1)
    def _():
        up.wait_send()
        down.wait_recv()

    @pl.when(me > 0)
    def _():
        down.wait_send()
        up.wait_recv()

    for b in range(HB):
        extended[b, 0:4] = sides[0, :, 128 * b : 128 * b + 128]
        extended[HB + blocks + b, 0:4] = sides[1, :, 128 * b : 128 * b + 128]
    for copy in copies:
        copy.wait()
    for i in range(1, tiles):
        other = lax.rem(me + i, tiles)
        got[other] = held[other]


def return_kernel(tiles, slopes, back, held, send_sem, recv_sem):
    me = lax.axis_index("tile")
    greet(tiles)
    copies = swap(tiles, slopes, held, send_sem, recv_sem)
    back[me] = slopes[me]
    for copy in copies:
        copy.wait()
    for i in range(1, tiles):
        other = lax.rem(me + i, tiles)
        back[other] = held[other]


def hot(index, length):
    return lax.broadcasted_iota(jnp.int32, (length, index.shape[1]), 0) == index


def halves(values):
    high = values.astype(jnp.bfloat16)
    low = (values - high.astype(jnp.float32)).astype(jnp.bfloat16)
    return high, low


def dot(a, b, contract):
    return lax.dot_general(
        a, b, ((contract[:1], contract[1:]), ((), ())), preferred_element_type=jnp.float32
    )


def pack_kernel(tiles, slot, sends, cells, out):
    width = slot + 128
    lane = lax.broadcasted_iota(jnp.int32, (2, slot), 1)
    start = jnp.int32(0)
    for d in range(tiles):
        n = sends[0, d]
        base = pl.multiple_of((start >> 7) << 7, 128)
        window = cells[:, pl.ds(base, width)]
        moved = pltpu.roll(window, width - (start - base), 1)
        out[d] = jnp.where(lane < n, moved[:2, :slot], 0.0)
        start = start + n


def unpack_kernel(tiles, slot, sends, back, force, out, padded, total):
    width = slot + 128
    capacity = out.shape[1]
    padded[...] = jnp.zeros_like(padded)
    total[...] = jnp.zeros_like(total)
    lane = lax.broadcasted_iota(jnp.int32, (8, width), 1)
    start = jnp.int32(0)
    for d in range(tiles):
        n = sends[0, d]
        base = pl.multiple_of((start >> 7) << 7, 128)
        shift = start - base
        padded[0:3, 0:slot] = back[d]
        moved = pltpu.roll(padded[...], shift, 1)
        there = jnp.logical_and(lane >= shift, lane < shift + n)
        total[:, pl.ds(base, width)] += jnp.where(there, moved, 0.0)
        start = start + n
    out[...] = FORCE_SCALE * force[0:3] + CHEMOTAXIS * total[0:3, 0:capacity]


def widen(table, wide):
    def one(e, carry):
        turned = jnp.transpose(table[e])
        for c in range(4):
            wide[e, c] = jnp.broadcast_to(turned[:, c : c + 1], (128, 128))
        return carry

    lax.fori_loop(0, table.shape[0], one, 0)


def force_blocks(chosen, table, wide, out, first, last):
    def one_block(b, carry):
        mine = table[b + HB]
        at = [jnp.broadcast_to(mine[c : c + 1], (8, 128)) for c in range(3)]

        def one_neighbour(k, sums):
            e = chosen[b, k]
            sx, sy, sz = sums
            for g in range(16):
                rows = slice(8 * g, 8 * g + 8)
                dx = at[0] - wide[e, 0, rows]
                dy = at[1] - wide[e, 1, rows]
                dz = at[2] - wide[e, 2, rows]
                far = jnp.exp(-0.25 * (dx * dx + dy * dy + dz * dz))
                square = far * far
                w = wide[e, 3, rows] * (REPULSION * (square * square) - ADHESION * far)
                sx = sx + w * dx
                sy = sy + w * dy
                sz = sz + w * dz
            return sx, sy, sz

        zero = jnp.zeros((8, 128), jnp.float32)
        sums = lax.fori_loop(0, K, one_neighbour, (zero, zero, zero))
        columns = pl.ds(pl.multiple_of(b * 128, 128), 128)
        for c in range(3):
            out[c : c + 1, columns] = mine[3:4] * jnp.sum(sums[c], axis=0, keepdims=True)
        return carry

    lax.fori_loop(first, last, one_block, 0)


def diffuse_kernel(
    slabs,
    tiles,
    chosen,
    table,
    start,
    out,
    force,
    edge_z,
    edge_y,
    state,
    wide,
    sent_y,
    halo_z,
    halo_y,
    send_sem,
    recv_sem,
):
    species, depth, rows, columns = start.shape
    slab, tile = lax.axis_index("slab"), lax.axis_index("tile")
    sides = (
        ("slab", slab, slabs, 0),
        ("slab", slab, slabs, 1),
        ("tile", tile, tiles, 0),
        ("tile", tile, tiles, 1),
    )

    def exists(side):
        axis, at, count, up = side
        return at < count - 1 if up else at > 0

    def partner(side):
        axis, at, count, up = side
        return {axis: jnp.minimum(at + 1, count - 1) if up else jnp.maximum(at - 1, 0)}

    halo_z[...] = jnp.zeros_like(halo_z)
    halo_y[...] = jnp.zeros_like(halo_y)
    barrier = pltpu.get_barrier_semaphore()
    for side in sides:

        @pl.when(exists(side))
        def _(side=side):
            pl.semaphore_signal(barrier, inc=1, device_id=partner(side), device_id_type=MESH)

    count = sum(exists(side).astype(jnp.int32) for side in sides)
    pl.semaphore_wait(barrier, count)

    def copies(step, now, which):
        made = []
        for n, side in enumerate(sides):
            up = side[3]
            if n < 2:
                source = state.at[now, which, depth if up else 1]
                target = halo_z.at[step, 1 - up, which]
            else:
                source = sent_y.at[step, up, which]
                target = halo_y.at[step, 1 - up, which]
            made.append(
                pltpu.make_async_remote_copy(
                    src_ref=source,
                    dst_ref=target,
                    send_sem=send_sem.at[step, n],
                    recv_sem=recv_sem.at[step, n],
                    device_id=partner(side),
                    device_id_type=MESH,
                )
            )
        return made

    def begin(step, now, which):
        made = copies(step, now, which)
        for n in (2, 3, 0, 1):

            @pl.when(exists(sides[n]))
            def _(n=n):
                made[n].start()

    def finish(step, now, which, axis):
        made = copies(step, now, which)
        for n in (2 * axis, 2 * axis + 1):

            @pl.when(exists(sides[n]))
            def _(n=n):
                made[n].wait_send()
                made[n ^ 1].wait_recv()

    blocks = force.shape[1] // 128
    share = blocks // (ITERS + 1)
    for now in range(2):
        for s in range(species):
            for z in (0, depth + 1):
                state[now, s, z] = jnp.zeros((rows, columns), jnp.float32)
    state[0, :, 1 : depth + 1] = start[...]
    lane = lax.broadcasted_iota(jnp.int32, (rows, columns), 1)
    row = lax.broadcasted_iota(jnp.int32, (rows, columns), 0)

    both = slice(0, species)
    for up in range(2):
        sent_y[0, up] = state[0, :, 1 : depth + 1, (rows - 1) * up, :]
    begin(0, 0, both)
    widen(table, wide)

    def settle(later, step, s, up, z):
        edge = slice((rows - 1) * up, (rows - 1) * up + 1)
        state[later, s, z, edge] = sent_y[step + 1, up, s, z - 1 : z]

    def one_step(step, after):
        now = lax.rem(step, 2)
        later = 1 - now
        for s in range(species):

            def one_plane(z, carry):
                c = state[now, s, z]
                around = state[now, s, z - 1] + state[now, s, z + 1]
                around += jnp.where(row == 0, 0.0, pltpu.roll(c, 1, 0))
                around += jnp.where(row == rows - 1, 0.0, pltpu.roll(c, rows - 1, 0))
                around += jnp.where(lane == 0, 0.0, pltpu.roll(c, 1, 1))
                around += jnp.where(lane == columns - 1, 0.0, pltpu.roll(c, columns - 1, 1))
                state[later, s, z] = c + DIFFUSION[s] * (around - 6.0 * c) - DECAY[s] * c
                return carry

            lax.fori_loop(1, depth + 1, one_plane, 0)
        force_blocks(chosen, table, wide, force, step * share, (step + 1) * share)
        for up in range(2):
            sent_y[step + 1, up] = state[later, :, 1 : depth + 1, (rows - 1) * up, :]
        finish(step, now, both, 0)
        for s in range(species):
            for side, z in enumerate((1, depth)):
                state[later, s, z] += DIFFUSION[s] * halo_z[step, side, s]
                for up in range(2):
                    edge = slice((rows - 1) * up, (rows - 1) * up + 1)
                    sent_y[step + 1, up, s, z - 1 : z] += (
                        DIFFUSION[s] * halo_z[step, side, s, edge]
                    )
        finish(step, now, both, 1)
        for s in range(species):
            for up in range(2):
                sent_y[step + 1, up, s] += DIFFUSION[s] * halo_y[step, up, s]
                for z in (1, depth):
                    settle(later, step, s, up, z)
        begin(step + 1, later, after)
        for s in range(species):
            for up in range(2):
                for z in range(2, depth):
                    settle(later, step, s, up, z)

    def earlier(step, carry):
        one_step(step, both)
        return carry

    lax.fori_loop(0, ITERS - 1, earlier, 0)
    one_step(jnp.int32(ITERS - 1), 1)
    last = ITERS % 2
    force_blocks(chosen, table, wide, force, ITERS * share, blocks)
    out[...] = state[last, :, 1 : depth + 1]
    finish(ITERS, last, 1, 0)
    finish(ITERS, last, 1, 1)
    edge_z[...] = halo_z[ITERS, :, 1]
    edge_y[...] = halo_y[ITERS, :, 1]


def deposit_kernel(got, field, out, oxygen, weights):
    tiles = got.shape[0]
    planes, columns = field.shape[1:]
    out[...] = field[...]
    high, low = halves(field[0])
    oxygen[0:planes] = high
    oxygen[planes:] = low

    def one_source(t, carry):
        wanted = got[t, 0:1].astype(jnp.int32)
        given = got[t, 1:2]
        row_hot = hot(wanted // columns, planes)
        lines = lax.broadcasted_iota(jnp.int32, (columns, wanted.shape[1]), 0).astype(jnp.int16)
        here = lines == (wanted % columns).astype(jnp.int16)
        column_hot = jnp.where(here, jnp.bfloat16(1), jnp.bfloat16(0))
        picked = dot(oxygen[...], column_hot, (1, 0))
        picked = picked[:planes] + picked[planes:]
        o = jnp.sum(jnp.where(row_hot, picked, 0.0), axis=0, keepdims=True)
        consume = given * o / (MICHAELIS_HALF + o)
        secrete = SECRETION * given * HYPOXIA_HALF / (HYPOXIA_HALF + o)
        for s, amount in enumerate((-STEP_TIME * consume, STEP_TIME * secrete)):
            high, low = halves(jnp.where(row_hot, amount, 0.0))
            weights[s * planes : (s + 1) * planes] = high
            weights[(s + 2) * planes : (s + 3) * planes] = low
        added = dot(weights[...], column_hot, (1, 1))
        for s in range(2):
            out[s] += (
                added[s * planes : (s + 1) * planes] + added[(s + 2) * planes : (s + 3) * planes]
            )
        return carry

    lax.fori_loop(0, tiles, one_source, 0, unroll=2)


def slope_kernel(depth, rows, got, field, edge_z, edge_y, out, near):
    tiles = got.shape[0]
    planes, columns = field.shape[1:]
    count = planes + 2 * rows + 2 * depth
    total = count + planes
    vegf = field[1]
    lane = lax.broadcasted_iota(jnp.int32, vegf.shape, 1)
    right = jnp.where(lane == columns - 1, 0.0, pltpu.roll(vegf, columns - 1, 1))
    left = jnp.where(lane == 0, 0.0, pltpu.roll(vegf, 1, 1))
    first = 0
    edges = jnp.concatenate([edge_y[0], edge_y[1]], axis=0)
    for part in (edge_z[0], vegf, edge_z[1], edges, right - left):
        high, low = halves(part)
        near[first : first + part.shape[0]] = high
        near[total + first : total + first + part.shape[0]] = low
        first += part.shape[0]

    def one_source(t, carry):
        wanted = got[t, 0:1].astype(jnp.int32)
        row = wanted // columns
        z, y = row // rows, row % rows
        column_hot = hot(wanted % columns, columns).astype(jnp.bfloat16)
        values = dot(near[...], column_hot, (1, 0))
        values = values[:total] + values[total:]
        change = jnp.where(hot(row, planes), values[count:], 0.0)
        values = values[:count]

        def at(index):
            return jnp.sum(jnp.where(hot(index, count), values, 0.0), axis=0, keepdims=True)

        below = jnp.where(y == 0, planes + 2 * rows + z, row + rows - 1)
        above = jnp.where(y == rows - 1, planes + 2 * rows + depth + z, row + rows + 1)
        out[t, 0:1] = 0.5 * (at(row + 2 * rows) - at(row))
        out[t, 1:2] = 0.5 * (at(above) - at(below))
        out[t, 2:3] = 0.5 * jnp.sum(change, axis=0, keepdims=True)
        return carry

    lax.fori_loop(0, tiles, one_source, 0, unroll=2)


def remote(number):
    return pltpu.CompilerParams(
        vmem_limit_bytes=48 * 1024 * 1024, collective_id=number, has_side_effects=True
    )


def shape_of(*shape):
    return jax.ShapeDtypeStruct(shape, jnp.float32)


def local(
    positions, radius, uptake_rate, voxel_local, cell_counts, send_counts, neighbor_blocks, field
):
    slabs, tiles = lax.axis_size("slab"), lax.axis_size("tile")
    capacity = positions.shape[1]
    slot = 2 * capacity // tiles
    blocks = capacity // 128
    species, depth, rows, columns = field.shape
    planes = depth * rows

    cells = jnp.stack([voxel_local.astype(jnp.float32), uptake_rate])
    cells = jnp.pad(cells, ((0, 6), (0, slot + 128)))
    packed = pl.pallas_call(
        functools.partial(pack_kernel, tiles, slot),
        out_shape=shape_of(tiles, 2, slot),
        in_specs=[SMEM, VMEM],
        out_specs=VMEM,
        compiler_params=LIMIT,
    )(send_counts, cells)
    cell = jnp.arange(capacity, dtype=jnp.int32)
    kept = jnp.where(cell < cell_counts[0], radius, 0.0)
    table = jnp.concatenate([positions, kept[None]], axis=0)
    got, extended = pl.pallas_call(
        functools.partial(meet_kernel, tiles),
        out_shape=(shape_of(tiles, 2, slot), shape_of(blocks + 2 * HB, 8, 128)),
        in_specs=[VMEM, VMEM],
        out_specs=[VMEM, VMEM],
        scratch_shapes=[
            pltpu.VMEM((tiles, 2, slot), jnp.float32),
            pltpu.VMEM((2, 4, HB * 128), jnp.float32),
            pltpu.SemaphoreType.DMA((tiles,)),
            pltpu.SemaphoreType.DMA((tiles,)),
            pltpu.SemaphoreType.DMA((4,)),
        ],
        compiler_params=remote(0),
    )(packed, table)

    state = pl.pallas_call(
        deposit_kernel,
        out_shape=shape_of(species, planes, columns),
        in_specs=[VMEM, VMEM],
        out_specs=VMEM,
        scratch_shapes=[
            pltpu.VMEM((2 * planes, columns), jnp.bfloat16),
            pltpu.VMEM((4 * planes, slot), jnp.bfloat16),
        ],
        compiler_params=LIMIT,
    )(got, field.reshape(species, planes, columns))
    steps = ITERS + 1
    state, force, edge_z, edge_y = pl.pallas_call(
        functools.partial(diffuse_kernel, slabs, tiles),
        out_shape=(
            shape_of(*field.shape),
            shape_of(8, capacity),
            shape_of(2, rows, columns),
            shape_of(2, depth, columns),
        ),
        in_specs=[SMEM, VMEM, VMEM],
        out_specs=[VMEM] * 4,
        scratch_shapes=[
            pltpu.VMEM((2, species, depth + 2, rows, columns), jnp.float32),
            pltpu.VMEM((blocks + 2 * HB, 4, 128, 128), jnp.float32),
            pltpu.VMEM((steps, 2, species, depth, columns), jnp.float32),
            pltpu.VMEM((steps, 2, species, rows, columns), jnp.float32),
            pltpu.VMEM((steps, 2, species, depth, columns), jnp.float32),
            pltpu.SemaphoreType.DMA((steps, 4)),
            pltpu.SemaphoreType.DMA((steps, 4)),
        ],
        compiler_params=remote(1),
    )(neighbor_blocks, extended, state.reshape(field.shape))

    slopes = pl.pallas_call(
        functools.partial(slope_kernel, depth, rows),
        out_shape=shape_of(tiles, 3, slot),
        in_specs=[VMEM] * 4,
        out_specs=VMEM,
        scratch_shapes=[
            pltpu.VMEM((4 * (planes + rows + depth), columns), jnp.bfloat16)
        ],
        compiler_params=LIMIT,
    )(got, state.reshape(species, planes, columns), edge_z, edge_y)
    back = pl.pallas_call(
        functools.partial(return_kernel, tiles),
        out_shape=shape_of(tiles, 3, slot),
        in_specs=[VMEM],
        out_specs=VMEM,
        scratch_shapes=[
            pltpu.VMEM((tiles, 3, slot), jnp.float32),
            pltpu.SemaphoreType.DMA((tiles,)),
            pltpu.SemaphoreType.DMA((tiles,)),
        ],
        compiler_params=remote(2),
    )(slopes)
    velocity = pl.pallas_call(
        functools.partial(unpack_kernel, tiles, slot),
        out_shape=shape_of(3, capacity),
        in_specs=[SMEM, VMEM, VMEM],
        out_specs=VMEM,
        scratch_shapes=[
            pltpu.VMEM((8, slot + 128), jnp.float32),
            pltpu.VMEM((8, capacity + slot + 128), jnp.float32),
        ],
        compiler_params=LIMIT,
    )(send_counts, back, force)
    return (velocity, state)


def solution(mesh):
    placed = (
        P(None, ("slab", "tile")),
        P(("slab", "tile")),
        P(("slab", "tile")),
        P(("slab", "tile")),
        P(("slab", "tile")),
        P(("slab", "tile"), None),
        P(("slab", "tile"), None),
        P(None, "slab", "tile", None),
    )
    return jax.shard_map(
        local,
        mesh=mesh,
        in_specs=placed,
        out_specs=(P(None, ("slab", "tile")), P(None, "slab", "tile", None)),
        check_vma=False,
    )
```
